32 devices in a mesh: groups: 2 (over x), tensor: 4 (over y, core), dp: 4 (over z).
Axes of the slice: x: 2, y: 2, z: 4, core: 2. Of those that a mesh axis runs over, the one named last changes fastest.
Arguments:
- hidden_states: bfloat16 [128, 2, 8192], P(('groups', 'tensor', 'dp')), parts along dimension 0, may hold values from -40 to 40
- norm_gain: bfloat16 [8192], replicated, may hold values from 0.099609375 to 1.8984375
- q_blocks: bfloat16 [64, 32, 128, 128], P('tensor'), may hold values from -0.09375 to 0.09375
- q_rows: int32 [64, 32], P('tensor'), may hold values from 0 to 63, as said below
- kv_blocks: bfloat16 [256, 128, 128], P('tensor'), may hold values from -0.09375 to 0.09375
- kv_rows: int32 [256], P('tensor'), may hold values from 0 to 63, as said below
- o_blocks: bfloat16 [64, 32, 128, 128], P('tensor'), may hold values from -0.75 to 0.75
- o_cols: int32 [64, 32], P('tensor'), may hold values from 0 to 63, as said below
- key_cache: bfloat16 [128, 1024, 512], P(('groups', 'tensor', 'dp')), parts along dimension 0, may hold values from -150 to 150
- value_cache: bfloat16 [128, 1024, 512], P(('groups', 'tensor', 'dp')), parts along dimension 0, may hold values from -4 to 4
- lengths: int32 [128], P(('groups', 'tensor', 'dp')), parts along dimension 0, may hold values from 1 to 1024, as said below
Outputs:
- attn_out: bfloat16 [128, 2, 8192], P(('groups', 'tensor', 'dp')), parts along dimension 0
- new_kv: bfloat16 [128, 2, 1024], P(('groups', 'tensor', 'dp')), parts along dimension 0
The draws below stay inside these ranges and needn't reach their ends.
There are 2 independent parts, one for each index of `groups`. The reference program is written for one: setup_inputs(seed, part) draws one part's arguments, and reference() takes and returns one part's arrays. A program takes and returns all parts, laid end to end along the dimension named above; an argument that names none is the same for every part. Nothing has to cross between parts.
Inputs may be any that keep to these rules, and one draw needn't show every extreme that they name: `q_rows`: each row lists 32 different feature blocks in ascending order. `kv_rows`: each aligned run of 32 entries lists 32 different feature blocks in ascending order. `o_cols`: each row lists 32 different column blocks in ascending order. `lengths`: some row has exactly 1024 cached positions and some row exactly 1.
All inputs are finite; a program needn't handle non-finite values.
Results may differ from the reference program's by a relative error of at most 0.007.
The reference program's roundings to bfloat16 on the way count: a program that leaves them out, or rounds other values in their place, can miss the bound.
Values may be sent and summed in bfloat16 or wider, within the bound.
A program may use at most 128 MiB of HBM per device.

```python
import math
import jax
import jax.numpy as jnp
from jax import lax

D = 8192
BLK = 128
QH = 64
KVH = 4
HD = 128
NEW = 2
ROW_DEV = 4
L = 1024
DB = 64
KEEP = 32
QCB = 64
KVCB = 8
ROWS = 64


def pick_blocks(key, line_count, block_count, keep_count):
    scores = jax.random.randint(key, (line_count, block_count), 0, 1 << 20) * block_count + jnp.arange(block_count, dtype=jnp.int32)[None, :]
    chosen = jnp.argsort(scores, axis=1)[:, :keep_count]
    return jnp.sort(chosen, axis=1).astype(jnp.int32)


def draw_q_rows(key, part):
    key = jax.random.fold_in(key, 11)
    return pick_blocks(key, QCB, DB, KEEP)


def draw_kv_rows(key, part):
    key = jax.random.fold_in(key, 12)
    return pick_blocks(key, KVCB, DB, KEEP).reshape(KVCB * KEEP)


def draw_o_cols(key, part):
    key = jax.random.fold_in(key, 13)
    return pick_blocks(key, QCB, DB, KEEP)


def draw_lengths(key, part):
    key = jax.random.fold_in(key, 14)
    draw_key, long_key, short_key = jax.random.split(key, 3)
    drawn = jax.random.randint(draw_key, (ROWS,), 1, L + 1)
    long_spot = jax.random.randint(long_key, (), 0, ROWS)
    short_spot = (long_spot + 1 + jax.random.randint(short_key, (), 0, ROWS - 1)) % ROWS
    return drawn.at[long_spot].set(L).at[short_spot].set(1).astype(jnp.int32)


def draw_hidden_states(key, part):
    key = jax.random.fold_in(key, 15)
    noise_key, row_key, col_key = jax.random.split(key, 3)
    noise_base = jnp.clip(jax.random.normal(noise_key, (ROWS, NEW, D)), -4.0, 4.0)
    row_scale = jnp.exp(jax.random.uniform(row_key, (ROWS, NEW, 1), minval=math.log(0.5), maxval=math.log(5.0)))
    col_scale = jnp.exp(jax.random.uniform(col_key, (D,), minval=math.log(0.5), maxval=math.log(5.0)))
    return jnp.clip(noise_base * row_scale * col_scale, -40.0, 40.0).astype(jnp.bfloat16)


def draw_key_cache(key, part):
    key = jax.random.fold_in(key, 16)
    noise_key = jax.random.fold_in(key, 0)
    noise_base = jnp.clip(jax.random.normal(noise_key, (ROWS, L, KVH * HD)), -4.0, 4.0)
    return jnp.clip(noise_base, -150.0, 150.0).astype(jnp.bfloat16)


def block_scale(key, dims, pieces, smallest, high):
    factor_of, own = 1.0, jax.random.fold_in(key, 6)
    for axis_at, shards_of in pieces:
        draws = jnp.exp(jax.random.uniform(jax.random.fold_in(own, axis_at), (shards_of,), jnp.float32, smallest / len(pieces), high / len(pieces)))
        factor_of = factor_of * jnp.repeat(draws, dims[axis_at] // shards_of).reshape([-1 if axis == axis_at else 1 for axis in range(len(dims))])
    return factor_of


def noise(rng, dims, width, most, cuts=(), kind=jnp.bfloat16):
    loudness = block_scale(rng, dims, cuts, -0.22, 0.18) if cuts else 1.0
    values = jax.random.normal(rng, dims, jnp.float32) * width * loudness
    return jnp.minimum(jnp.maximum(values, -most), most).astype(kind)


def setup_inputs(seed: int = 0, part: int = 0) -> dict:
    arg_keys = jax.random.split(jax.random.key(seed), 12)
    own_keys = jax.random.split(jax.random.fold_in(arg_keys[11], part), 12)
    return {
        "hidden_states": draw_hidden_states(jax.random.fold_in(jax.random.fold_in(arg_keys[11], part), 71), part),
        "norm_gain": jnp.clip(1.0 + 0.18 * jax.random.normal(arg_keys[1], (D,), jnp.float32), 0.099609375, 1.8984375).astype(jnp.bfloat16),
        "q_blocks": noise(arg_keys[2], (QCB, KEEP, BLK, BLK), (D // 2) ** -0.5, 0.09375, ((0, 4),)),
        "q_rows": draw_q_rows(jax.random.fold_in(arg_keys[11], 71), part),
        "kv_blocks": noise(arg_keys[4], (KVCB * KEEP, BLK, BLK), (D // 2) ** -0.5, 0.09375, ((0, 4),)),
        "kv_rows": draw_kv_rows(jax.random.fold_in(arg_keys[11], 71), part),
        "o_blocks": noise(arg_keys[6], (QCB, KEEP, BLK, BLK), (max(KEEP * BLK // 64, 1)) ** -0.5, 0.75, ((0, 4),)),
        "o_cols": draw_o_cols(jax.random.fold_in(arg_keys[11], 71), part),
        "key_cache": draw_key_cache(jax.random.fold_in(jax.random.fold_in(arg_keys[11], part), 71), part),
        "value_cache": noise(own_keys[9], (ROWS, L, KVH * HD), 1.0, 4.0, ((0, 16),)),
        "lengths": draw_lengths(jax.random.fold_in(jax.random.fold_in(arg_keys[11], part), 71), part),
    }


def normalize(states, gain):
    widened = states.astype(jnp.float32)
    inv_rms = lax.rsqrt(lax.optimization_barrier(jnp.mean(widened * widened, axis=-1, keepdims=True)) + 1e-05)
    return (widened * inv_rms * gain.astype(jnp.float32)).astype(jnp.bfloat16)

def rotate(vectors, positions):
    half_width = vectors.shape[-1] // 2
    frequency = 500000.0 ** (-jnp.arange(half_width, dtype=jnp.float32) / half_width)
    angles = positions[..., None] * frequency
    cosine = jnp.cos(angles)
    sine_part = jnp.sin(angles)
    lower_half = vectors[..., :half_width]
    upper_half = vectors[..., half_width:]
    return jnp.concatenate([lower_half * cosine - upper_half * sine_part, upper_half * cosine + lower_half * sine_part], axis=-1)

def column_blocks(blocks_in, blocks, row_ids):

    def one_column(operands):
        weight, picks = operands
        picked = jnp.take(blocks_in, picks.astype(jnp.int32), axis=1).astype(jnp.float32)
        return jnp.einsum('tkb,kbc->tc', picked, weight.astype(jnp.float32))
    summed = lax.map(one_column, (blocks, row_ids))
    return jnp.transpose(summed, (1, 0, 2)).reshape(summed.shape[1], summed.shape[0] * summed.shape[2])

def attend(queries, fresh_kv, key_cache, value_cache, lengths):
    own_rows = queries.shape[0]
    cache_len = key_cache.shape[1]
    group_size = QH // KVH
    scale = HD ** (-0.5)
    highest = lax.Precision.HIGHEST
    query_f = queries.reshape(own_rows, NEW, KVH, group_size, HD).astype(jnp.float32)
    cache_keys = key_cache.reshape(own_rows, cache_len, KVH, HD).astype(jnp.float32)
    cache_values = value_cache.reshape(own_rows, cache_len, KVH, HD).astype(jnp.float32)
    fresh_keys = fresh_kv[..., :KVH * HD].reshape(own_rows, NEW, KVH, HD).astype(jnp.float32)
    fresh_values = fresh_kv[..., KVH * HD:].reshape(own_rows, NEW, KVH, HD).astype(jnp.float32)
    cached = jnp.einsum('rjkgd,rpkd->rjkgp', query_f, cache_keys, precision=highest) * scale
    recent = jnp.einsum('rjkgd,rikd->rjkgi', query_f, fresh_keys, precision=highest) * scale
    is_valid = (jnp.arange(cache_len, dtype=jnp.int32)[None, :] < lengths.astype(jnp.int32)[:, None])[:, None, None, None, :]
    steps_new = jnp.arange(NEW, dtype=jnp.int32)
    causal = (steps_new[None, :] <= steps_new[:, None])[None, :, None, None, :]
    row_max = jnp.maximum(lax.optimization_barrier(jnp.max(jnp.where(is_valid, cached, -1e+30), axis=-1)), lax.optimization_barrier(jnp.max(jnp.where(causal, recent, -1e+30), axis=-1)))
    cache_weights = jnp.where(is_valid, jnp.exp(cached - row_max[..., None]), 0.0).astype(jnp.bfloat16).astype(jnp.float32)
    fresh_weights = jnp.where(causal, jnp.exp(recent - row_max[..., None]), 0.0).astype(jnp.bfloat16).astype(jnp.float32)
    denominator = lax.optimization_barrier(jnp.sum(cache_weights, axis=-1)) + lax.optimization_barrier(jnp.sum(fresh_weights, axis=-1))
    numerator = jnp.einsum('rjkgp,rpkd->rjkgd', cache_weights, cache_values, precision=highest)
    numerator = numerator + jnp.einsum('rjkgi,rikd->rjkgd', fresh_weights, fresh_values, precision=highest)
    return (numerator / denominator[..., None]).reshape(own_rows, NEW, QH * HD).astype(jnp.bfloat16)

def reference(hidden_states, norm_gain, q_blocks, q_rows, kv_blocks, kv_rows, o_blocks, o_cols, key_cache, value_cache, lengths):
    tokens = ROWS * NEW
    normed = normalize(hidden_states, norm_gain)
    blocks_in = normed.reshape(tokens, DB, BLK)
    queries_raw = lax.optimization_barrier(column_blocks(blocks_in, q_blocks, q_rows).astype(jnp.bfloat16))
    kv_raw = column_blocks(blocks_in, kv_blocks.reshape(KVCB, KEEP, BLK, BLK), kv_rows.reshape(KVCB, KEEP))
    positions = (lengths.astype(jnp.int32)[:, None] + jnp.arange(NEW, dtype=jnp.int32)[None, :]).astype(jnp.float32)
    queries = rotate(queries_raw.astype(jnp.float32).reshape(ROWS, NEW, QH, HD), positions[..., None]).astype(jnp.bfloat16)
    keys_new = rotate(kv_raw[:, :KVH * HD].reshape(ROWS, NEW, KVH, HD), positions[..., None])
    new_kv = jnp.concatenate([keys_new.reshape(ROWS, NEW, KVH * HD), kv_raw[:, KVH * HD:].reshape(ROWS, NEW, KVH * HD)], axis=-1).astype(jnp.bfloat16)
    row_blocks = ROWS // ROW_DEV

    def attend_block(operands):
        return attend(*operands)
    attended = lax.map(attend_block, (queries.reshape(row_blocks, ROW_DEV, NEW, QH, HD), new_kv.reshape(row_blocks, ROW_DEV, NEW, 2 * KVH * HD), key_cache.reshape(row_blocks, ROW_DEV, L, KVH * HD), value_cache.reshape(row_blocks, ROW_DEV, L, KVH * HD), lengths.reshape(row_blocks, ROW_DEV)))
    o_in = attended.reshape(tokens, QCB, BLK)

    def add_block(summed, operands):
        block_in, weight, col_ids = operands
        contrib = jnp.einsum('tb,kbc->tkc', block_in.astype(jnp.float32), weight.astype(jnp.float32))
        onehot = (col_ids.astype(jnp.int32)[:, None] == jnp.arange(DB, dtype=jnp.int32)[None, :]).astype(jnp.float32)
        return (summed + jnp.einsum('tkc,kn->tnc', contrib, onehot, precision=lax.Precision.HIGHEST), None)
    summed, _ = lax.scan(add_block, jnp.zeros((tokens, DB, BLK), jnp.float32), (jnp.transpose(o_in, (1, 0, 2)), o_blocks, o_cols))
    attn_out = summed.reshape(ROWS, NEW, D).astype(jnp.bfloat16)
    return (attn_out, new_kv)
```

```python
import functools

import jax
import jax.numpy as jnp
from jax import lax
from jax.experimental import pallas as pl
from jax.experimental.pallas import tpu as pltpu
from jax.sharding import PartitionSpec as P

D = 8192
BLK = 128
QH = 64
KVH = 4
HD = 128
NEW = 2
DB = 64
KEEP = 32
KVCB = 8
ROW_DEV = 4
OWN = ROW_DEV * NEW
GROUP = QH // KVH
PAD = 128
CHUNKS = 8
MESH = pl.DeviceIdType.MESH
F32 = jnp.float32
BF16 = jnp.bfloat16


def kernel(
    tp,
    hh,
    entries,
    cache_len,
    hidden,
    gain,
    cosine,
    sine,
    q_rows,
    kv_rows,
    place,
    lengths,
    q_hbm,
    kv_hbm,
    o_hbm,
    k_hbm,
    v_hbm,
    out,
    new_kv,
    wq,
    wkv,
    wo,
    kbuf,
    vbuf,
    nf,
    xg,
    qs,
    qr,
    qf,
    ks,
    kr,
    af,
    asend,
    ar,
    xo,
    pbuf,
    rbuf,
    sbuf,
    fbuf,
    q_sem,
    kv_sem,
    o_sem,
    c_sem,
    x1_sem,
    x2_sem,
    x3_sem,
    qa_sem,
    ka_sem,
    aa_sem,
    s1_sem,
    s2_sem,
):
    ny = tp // 2
    me = lax.axis_index("tensor")
    my = me // 2
    mc = lax.rem(me, 2)
    other = my * 2 + (1 - mc)

    q_copies = [pltpu.make_async_copy(q_hbm.at[c], wq.at[c], q_sem.at[c]) for c in range(hh)]
    kv_copy = pltpu.make_async_copy(kv_hbm, wkv, kv_sem)
    k_copies = [
        pltpu.make_async_copy(k_hbm.at[r], kbuf.at[r, pl.ds(0, cache_len)], c_sem.at[0, r])
        for r in range(ROW_DEV)
    ]
    v_copies = [
        pltpu.make_async_copy(v_hbm.at[r], vbuf.at[r, pl.ds(0, cache_len)], c_sem.at[1, r])
        for r in range(ROW_DEV)
    ]
    o_copies = [
        pltpu.make_async_copy(o_hbm.at[i], wo.at[pl.ds(i * KEEP, KEEP)], o_sem.at[i])
        for i in range(hh)
    ]
    kv_copy.start()
    for copy in q_copies + k_copies + v_copies + o_copies:
        copy.start()

    def remote(src, dst, sems, slot, target):
        return pltpu.make_async_remote_copy(
            src_ref=src,
            dst_ref=dst,
            send_sem=sems.at[(0,) + slot],
            recv_sem=sems.at[(1,) + slot],
            device_id={"tensor": target},
            device_id_type=MESH,
        )

    barrier = pltpu.get_barrier_semaphore()
    for step in range(1, tp):
        pl.semaphore_signal(
            barrier, inc=1, device_id={"tensor": lax.rem(me + step, tp)}, device_id_type=MESH
        )

    wide = hidden[...].astype(F32)
    inv_rms = lax.rsqrt(jnp.mean(wide * wide, axis=-1, keepdims=True) + 1e-05)
    normed = (wide * inv_rms * gain[...].astype(F32)).astype(BF16).astype(F32)
    for b in range(DB):
        nf[mc, b] = normed[:, b * BLK : (b + 1) * BLK]
    wo[hh * KEEP] = jnp.zeros((BLK, BLK), BF16)

    pl.semaphore_wait(barrier, tp - 1)

    x1 = remote(nf.at[mc], nf.at[mc], x1_sem, (0,), other)
    x1.start()
    x1_in = remote(nf.at[1 - mc], nf.at[1 - mc], x1_sem, (0,), other)
    x1_in.wait_recv()
    xg[my] = jnp.concatenate([nf[0], nf[1]], axis=1).astype(BF16)

    half = DB // 2
    mine = pl.ds(mc * half, half)
    theirs = pl.ds((1 - mc) * half, half)
    x2 = []
    for step in range(1, ny):
        to = lax.rem(my + step, ny)
        copy = remote(xg.at[my, mine], xg.at[my, mine], x2_sem, (step,), to * 2 + mc)
        copy.start()
        x2.append(copy)
    x3 = []
    for step in range(1, ny):
        source = lax.rem(my + ny - step, ny)
        piece = xg.at[source, mine]
        remote(piece, piece, x2_sem, (step,), other).wait_recv()
        copy = remote(piece, piece, x3_sem, (step,), other)
        copy.start()
        x3.append(copy)
    for step in range(1, ny):
        source = lax.rem(my + ny - step, ny)
        piece = xg.at[source, theirs]
        remote(piece, piece, x3_sem, (step,), other).wait_recv()

    def picked(rows):
        blocks = [jnp.concatenate([xg[y, row] for y in range(ny)], axis=0) for row in rows]
        return jnp.concatenate(blocks, axis=1)

    kv_copy.wait()
    cols = max(1, entries // KEEP)
    per = entries // cols
    for col in range(cols):
        x = picked([kv_rows[col * per + e] for e in range(per)])
        w = wkv[pl.ds(col * per, per)].reshape(per * BLK, BLK)
        part = jnp.dot(x, w, preferred_element_type=F32)
        for d in range(tp):
            ks[d, pl.ds(col * OWN, OWN)] = part[d * OWN : (d + 1) * OWN]
    sends = []
    for step in range(1, tp):
        to = lax.rem(me + step, tp)
        copy = remote(ks.at[to], kr.at[me], ka_sem, (step,), to)
        copy.start()
        sends.append(copy)
    kr[me] = ks[me]

    for copy in q_copies:
        copy.wait()

    def query_pair(pair, carry):
        parts = []
        for s in range(2):
            c = pair * 2 + s
            x = picked([q_rows[c * KEEP + k] for k in range(KEEP)])
            w = wq[c].reshape(KEEP * BLK, BLK)
            parts.append(jnp.dot(x, w, preferred_element_type=F32))
        for d in range(tp):
            both = jnp.concatenate([p[d * OWN : (d + 1) * OWN] for p in parts], axis=0)
            qs[d, pl.ds(pl.multiple_of(pair * 16, 16), 16)] = both.astype(BF16)
        return carry

    lax.fori_loop(0, hh // 2, query_pair, 0)
    slab = hh * OWN
    for step in range(1, tp):
        to = lax.rem(me + step, tp)
        copy = remote(qs.at[to], qr.at[me], qa_sem, (step,), to)
        copy.start()
        sends.append(copy)
    qr[me] = qs[me]

    cos_own = cosine[...]
    sin_own = sine[...]
    for step in range(1, tp):
        source = lax.rem(me + tp - step, tp)
        remote(ks.at[source], kr.at[source], ka_sem, (step,), source).wait_recv()
    share = max(1, KEEP // entries)
    fresh = []
    for col in range(KVCB):
        if share == 1:
            total = kr[col // cols, pl.ds((col % cols) * OWN, OWN)]
        else:
            total = kr[col * share]
            for extra in range(1, share):
                total = total + kr[col * share + extra]
        if col < KVH:
            total = total * cos_own + pltpu.roll(total, HD // 2, 1) * sin_own
        fresh.append(total)
    fresh = jnp.concatenate(fresh, axis=1).astype(BF16)
    new_kv[...] = fresh
    tail = jnp.concatenate(
        [fresh.astype(F32), jnp.zeros((PAD - OWN, 2 * KVH * HD), F32)], axis=0
    ).astype(BF16)
    for r in range(ROW_DEV):
        kbuf[r, pl.ds(cache_len, PAD)] = tail[:, : KVH * HD]
        vbuf[r, pl.ds(cache_len, PAD)] = tail[:, KVH * HD :]

    for step in range(1, tp):
        source = lax.rem(me + tp - step, tp)
        remote(qs.at[source], qr.at[source], qa_sem, (step,), source).wait_recv()
    for s in range(tp):
        raw = qr[s].astype(F32)
        swapped = pltpu.roll(raw, HD // 2, 1)
        turned = raw.reshape(hh, OWN, HD) * cos_own[None] + swapped.reshape(hh, OWN, HD) * sin_own[None]
        qf[pl.ds(s * slab, slab)] = turned.reshape(slab, HD)
    for copy in k_copies + v_copies:
        copy.wait()

    width = cache_len + PAD
    scale = HD ** (-0.5)
    spot = lax.broadcasted_iota(jnp.int32, (NEW * GROUP, width), 1)
    token = lax.broadcasted_iota(jnp.int32, (NEW * GROUP, width), 0) // GROUP

    def attend_row(r, carry):
        first = cache_len + NEW * r
        valid = (spot < lengths[r]) | ((spot >= first) & (spot <= first + token))
        for g in range(KVH):
            q = jnp.concatenate(
                [qf[pl.ds(g * GROUP * OWN + NEW * r + j, GROUP, stride=OWN)] for j in range(NEW)],
                axis=0,
            ).astype(BF16)
            keys = kbuf[r, :, g * HD : (g + 1) * HD]
            scores = lax.dot_general(
                q, keys, (((1,), (1,)), ((), ())), preferred_element_type=F32
            )
            scores = jnp.where(valid, scores * scale, -1e30)
            top = jnp.max(scores, axis=-1, keepdims=True)
            weights = jnp.where(valid, jnp.exp(scores - top), 0.0).astype(BF16)
            below = jnp.sum(weights.astype(F32), axis=-1, keepdims=True)
            values = vbuf[r, :, g * HD : (g + 1) * HD]
            above = jnp.dot(weights, values, preferred_element_type=F32)
            result = above / below
            for j in range(NEW):
                af[pl.ds(g * GROUP * OWN + NEW * r + j, GROUP, stride=OWN)] = result[
                    j * GROUP : (j + 1) * GROUP
                ]
        return carry

    lax.fori_loop(0, ROW_DEV, attend_row, 0)

    for d in range(tp):
        asend[d] = af[pl.ds(d * slab, slab)].astype(BF16)
    for step in range(1, tp):
        to = lax.rem(me + step, tp)
        copy = remote(asend.at[to], ar.at[me], aa_sem, (step,), to)
        copy.start()
        sends.append(copy)
    ar[me] = asend[me]
    for copy in o_copies:
        copy.wait()
    for step in range(1, tp):
        source = lax.rem(me + tp - step, tp)
        remote(asend.at[source], ar.at[source], aa_sem, (step,), source).wait_recv()

    order = [y * 2 + c for c in range(2) for y in range(ny)]
    heads = [ar[s].astype(F32) for s in order]
    for i in range(hh):
        lhs = jnp.concatenate([h[i * OWN : (i + 1) * OWN] for h in heads], axis=0)
        xo[:, i * BLK : (i + 1) * BLK] = lhs.astype(BF16)

    pairs = DB // CHUNKS // 2
    side = ny * OWN

    def stage1(ch):
        return remote(pbuf.at[ch, 1 - mc], rbuf.at[ch], s1_sem, (ch,), other)

    def stage2(ch, step):
        to = lax.rem(my + step, ny)
        piece = sbuf.at[ch, pl.ds(pl.multiple_of(to * OWN, OWN), OWN)]
        return remote(piece, fbuf.at[ch, my], s2_sem, (ch, step), to * 2 + mc)

    def pass_on(ch):
        stage1(ch).wait_recv()
        sbuf[ch] = pbuf[ch, mc] + rbuf[ch]
        for step in range(1, ny):
            stage2(ch, step).start()

    def project(ch, carry):
        def one_pair(pair, inner):
            n = (ch * pairs + pair) * 2
            total = None
            wide_k = 2 if hh % 2 == 0 else 1
            for i in range(0, hh, wide_k):
                w = jnp.concatenate(
                    [
                        jnp.concatenate(
                            [wo[place[(n + a) * hh + i + b]] for b in range(wide_k)], axis=0
                        )
                        for a in range(2)
                    ],
                    axis=1,
                )
                part = jnp.dot(
                    xo[:, i * BLK : (i + wide_k) * BLK], w, preferred_element_type=F32
                )
                total = part if total is None else total + part
            columns = pl.ds(pl.multiple_of(pair * 2 * BLK, 2 * BLK), 2 * BLK)
            for c in range(2):
                pbuf[ch, c, :, columns] = total[c * side : (c + 1) * side]
            return inner

        lax.fori_loop(0, pairs, one_pair, 0)
        stage1(ch).start()

        @pl.when(ch > 0)
        def _():
            pass_on(ch - 1)

        return carry

    lax.fori_loop(0, CHUNKS, project, 0)
    pass_on(CHUNKS - 1)

    def finish(ch, carry):
        total = sbuf[ch, pl.ds(pl.multiple_of(my * OWN, OWN), OWN)]
        for step in range(1, ny):
            source = lax.rem(my + ny - step, ny)
            remote(
                sbuf.at[ch, pl.ds(0, OWN)], fbuf.at[ch, source], s2_sem, (ch, step), other
            ).wait_recv()
            total = total + fbuf[ch, source]
        wide_chunk = D // CHUNKS
        out[:, pl.ds(pl.multiple_of(ch * wide_chunk, wide_chunk), wide_chunk)] = total.astype(BF16)
        return carry

    lax.fori_loop(0, CHUNKS, finish, 0)

    x1.wait_send()
    for copy in x2 + x3 + sends:
        copy.wait_send()

    def drain(ch, carry):
        stage1(ch).wait_send()
        for step in range(1, ny):
            stage2(ch, step).wait_send()
        return carry

    lax.fori_loop(0, CHUNKS, drain, 0)


def on_device(
    tp,
    hidden_states,
    norm_gain,
    q_blocks,
    q_rows,
    kv_blocks,
    kv_rows,
    o_blocks,
    o_cols,
    key_cache,
    value_cache,
    lengths,
):
    hh = q_blocks.shape[0]
    entries = kv_blocks.shape[0]
    cache_len = key_cache.shape[1]
    ny = tp // 2
    half = HD // 2
    frequency = 500000.0 ** (-jnp.arange(half, dtype=F32) / half)
    positions = (lengths[:, None] + jnp.arange(NEW, dtype=jnp.int32)[None, :]).astype(F32)
    angles = positions.reshape(OWN, 1) * frequency
    cos_half, sin_half = jnp.cos(angles), jnp.sin(angles)
    cosine = jnp.concatenate([cos_half, cos_half], axis=-1)
    sine = jnp.concatenate([-sin_half, sin_half], axis=-1)
    slot = jnp.arange(hh * KEEP, dtype=jnp.int32).reshape(hh, KEEP)
    hit = o_cols[None] == jnp.arange(DB, dtype=jnp.int32)[:, None, None]
    place = jnp.min(jnp.where(hit, slot[None], hh * KEEP), axis=-1).reshape(DB * hh)

    vmem = pl.BlockSpec(memory_space=pltpu.VMEM)
    smem = pl.BlockSpec(memory_space=pltpu.SMEM)
    anywhere = pl.BlockSpec(memory_space=pl.ANY)
    slab = hh * OWN
    cols = max(1, entries // KEEP)
    width = cache_len + PAD
    chunk = D // CHUNKS
    dma = pltpu.SemaphoreType.DMA
    out, new_kv = pl.pallas_call(
        functools.partial(kernel, tp, hh, entries, cache_len),
        out_shape=(
            jax.ShapeDtypeStruct((OWN, D), BF16),
            jax.ShapeDtypeStruct((OWN, 2 * KVH * HD), BF16),
        ),
        in_specs=[vmem] * 4 + [smem] * 4 + [anywhere] * 5,
        out_specs=(vmem, vmem),
        scratch_shapes=[
            pltpu.VMEM((hh, KEEP, BLK, BLK), BF16),
            pltpu.VMEM((entries, BLK, BLK), BF16),
            pltpu.VMEM((hh * KEEP + 1, BLK, BLK), BF16),
            pltpu.VMEM((ROW_DEV, width, KVH * HD), BF16),
            pltpu.VMEM((ROW_DEV, width, KVH * HD), BF16),
            pltpu.VMEM((2, DB, OWN, BLK), F32),
            pltpu.VMEM((ny, DB, 2 * OWN, BLK), BF16),
            pltpu.VMEM((tp, slab, HD), BF16),
            pltpu.VMEM((tp, slab, HD), BF16),
            pltpu.VMEM((tp * slab, HD), F32),
            pltpu.VMEM((tp, cols * OWN, BLK), F32),
            pltpu.VMEM((tp, cols * OWN, BLK), F32),
            pltpu.VMEM((tp * slab, HD), F32),
            pltpu.VMEM((tp, slab, HD), BF16),
            pltpu.VMEM((tp, slab, HD), BF16),
            pltpu.VMEM((tp * OWN, hh * BLK), BF16),
            pltpu.VMEM((CHUNKS, 2, ny * OWN, chunk), F32),
            pltpu.VMEM((CHUNKS, ny * OWN, chunk), F32),
            pltpu.VMEM((CHUNKS, ny * OWN, chunk), F32),
            pltpu.VMEM((CHUNKS, ny, OWN, chunk), F32),
            dma((hh,)),
            dma,
            dma((hh,)),
            dma((2, ROW_DEV)),
            dma((2, 1)),
            dma((2, ny)),
            dma((2, ny)),
            dma((2, tp)),
            dma((2, tp)),
            dma((2, tp)),
            dma((2, CHUNKS)),
            dma((2, CHUNKS, ny)),
        ],
        compiler_params=pltpu.CompilerParams(
            collective_id=0, has_side_effects=True, vmem_limit_bytes=60 * 1024 * 1024
        ),
    )(
        hidden_states.reshape(OWN, D),
        norm_gain.reshape(1, D),
        cosine,
        sine,
        q_rows.reshape(hh * KEEP),
        kv_rows,
        place,
        lengths,
        q_blocks,
        kv_blocks,
        o_blocks,
        key_cache,
        value_cache,
    )
    return out.reshape(ROW_DEV, NEW, D), new_kv.reshape(ROW_DEV, NEW, 2 * KVH * HD)


def solution(mesh):
    rows = P(("groups", "tensor", "dp"), None, None)
    return jax.shard_map(
        functools.partial(on_device, mesh.shape["tensor"]),
        mesh=mesh,
        in_specs=(
            rows,
            P(),
            P("tensor", None, None, None),
            P("tensor", None),
            P("tensor", None, None),
            P("tensor"),
            P("tensor", None, None, None),
            P("tensor", None),
            rows,
            rows,
            P(("groups", "tensor", "dp")),
        ),
        out_specs=(rows, rows),
        check_vma=False,
    )
```

```python
import functools
import math

import jax
import jax.numpy as jnp
from jax import lax
from jax.experimental import pallas as pl
from jax.experimental.pallas import tpu as pltpu
from jax.sharding import PartitionSpec as P

D = 8192
BLK = 128
QH = 64
KVH = 4
HD = 128
NEW = 2
DB = 64
KEEP = 32
KVCB = 8
ROW_DEV = 4
OWN = ROW_DEV * NEW
GROUP = QH // KVH
PAD = 128
CHUNKS = 8
MESH = pl.DeviceIdType.MESH
F32 = jnp.float32
BF16 = jnp.bfloat16


def kernel(
    tp,
    hh,
    entries,
    cache_len,
    hidden,
    gain,
    q_rows,
    kv_rows,
    o_cols,
    lengths,
    q_hbm,
    kv_hbm,
    o_hbm,
    k_hbm,
    v_hbm,
    out,
    new_kv,
    wq,
    wkv,
    wo,
    kbuf,
    vbuf,
    nf,
    xg,
    qs,
    qr,
    qf,
    ks,
    kr,
    af,
    asend,
    ar,
    xo,
    pbuf,
    rbuf,
    sbuf,
    fbuf,
    reached,
    q_sem,
    kv_sem,
    o_sem,
    c_sem,
    x1_sem,
    x2_sem,
    x3_sem,
    qa_sem,
    ka_sem,
    aa_sem,
    s1_sem,
    s2_sem,
):
    ny = tp // 2
    me = lax.axis_index("tensor")
    my = me // 2
    mc = lax.rem(me, 2)
    other = my * 2 + (1 - mc)

    q_copies = [pltpu.make_async_copy(q_hbm.at[c], wq.at[c], q_sem.at[c]) for c in range(hh)]
    kv_copy = pltpu.make_async_copy(kv_hbm, wkv, kv_sem)
    k_copies = [
        pltpu.make_async_copy(k_hbm.at[r], kbuf.at[r, pl.ds(0, cache_len)], c_sem.at[0, r])
        for r in range(ROW_DEV)
    ]
    v_copies = [
        pltpu.make_async_copy(v_hbm.at[r], vbuf.at[r, pl.ds(0, cache_len)], c_sem.at[1, r])
        for r in range(ROW_DEV)
    ]
    o_copies = [
        pltpu.make_async_copy(o_hbm.at[i], wo.at[pl.ds(i * KEEP, KEEP)], o_sem.at[i])
        for i in range(hh)
    ]
    kv_copy.start()
    for copy in q_copies:
        copy.start()

    def remote(src, dst, sems, slot, target):
        return pltpu.make_async_remote_copy(
            src_ref=src,
            dst_ref=dst,
            send_sem=sems.at[(0,) + slot],
            recv_sem=sems.at[(1,) + slot],
            device_id={"tensor": target},
            device_id_type=MESH,
        )

    barrier = pltpu.get_barrier_semaphore()
    for step in range(1, tp):
        pl.semaphore_signal(
            barrier, inc=1, device_id={"tensor": lax.rem(me + step, tp)}, device_id_type=MESH
        )

    wide = jnp.concatenate([hidden[r].astype(F32) for r in range(ROW_DEV)], axis=0)
    inv_rms = lax.rsqrt(jnp.mean(wide * wide, axis=-1, keepdims=True) + 1e-05)
    normed = (wide * inv_rms * gain[...].astype(F32).reshape(1, D)).astype(BF16).astype(F32)
    for b in range(DB):
        nf[mc, b] = normed[:, b * BLK : (b + 1) * BLK]
    wo[hh * KEEP] = jnp.zeros((BLK, BLK), BF16)

    lane = lax.broadcasted_iota(jnp.int32, (OWN, HD), 1)
    row = lax.broadcasted_iota(jnp.int32, (OWN, HD), 0)
    position = lax.rem(row, NEW)
    for r in range(ROW_DEV):
        position = position + jnp.where(row // NEW == r, lengths[r], 0)
    exponent = lax.rem(lane, HD // 2).astype(F32) * (-math.log(500000.0) / (HD // 2))
    angles = position.astype(F32) * jnp.exp(exponent)
    cos_own = jnp.cos(angles)
    sin_own = jnp.sin(angles)
    sin_own = jnp.where(lane < HD // 2, -sin_own, sin_own)

    pl.semaphore_wait(barrier, tp - 1)

    x1 = remote(nf.at[mc], nf.at[mc], x1_sem, (0,), other)
    x1.start()
    for copy in k_copies + v_copies:
        copy.start()
    x1_in = remote(nf.at[1 - mc], nf.at[1 - mc], x1_sem, (0,), other)
    x1_in.wait_recv()
    xg[my] = jnp.concatenate([nf[0], nf[1]], axis=1).astype(BF16)

    half = DB // 2
    mine = pl.ds(mc * half, half)
    theirs = pl.ds((1 - mc) * half, half)
    x2 = []
    for step in range(1, ny):
        to = lax.rem(my + step, ny)
        copy = remote(xg.at[my, mine], xg.at[my, mine], x2_sem, (step,), to * 2 + mc)
        copy.start()
        x2.append(copy)
    x3 = []
    for step in range(1, ny):
        source = lax.rem(my + ny - step, ny)
        piece = xg.at[source, mine]
        remote(piece, piece, x2_sem, (step,), other).wait_recv()
        copy = remote(piece, piece, x3_sem, (step,), other)
        copy.start()
        x3.append(copy)
    for step in range(1, ny):
        source = lax.rem(my + ny - step, ny)
        piece = xg.at[source, theirs]
        remote(piece, piece, x3_sem, (step,), other).wait_recv()

    def picked(rows):
        blocks = [jnp.concatenate([xg[y, row] for y in range(ny)], axis=0) for row in rows]
        return jnp.concatenate(blocks, axis=1)

    kv_copy.wait()
    cols = max(1, entries // KEEP)
    per = entries // cols
    for col in range(cols):
        x = picked([kv_rows[col * per + e] for e in range(per)])
        w = wkv[pl.ds(col * per, per)].reshape(per * BLK, BLK)
        part = jnp.dot(x, w, preferred_element_type=F32)
        for d in range(tp):
            ks[d, pl.ds(col * OWN, OWN)] = part[d * OWN : (d + 1) * OWN]
    sends = []
    for step in range(1, tp):
        to = lax.rem(me + step, tp)
        copy = remote(ks.at[to], kr.at[me], ka_sem, (step,), to)
        copy.start()
        sends.append(copy)
    kr[me] = ks[me]

    for copy in q_copies:
        copy.wait()
    for copy in o_copies:
        copy.start()

    def query_pair(pair, carry):
        parts = []
        for s in range(2):
            c = pair * 2 + s
            x = picked([q_rows[c, k] for k in range(KEEP)])
            w = wq[c].reshape(KEEP * BLK, BLK)
            parts.append(jnp.dot(x, w, preferred_element_type=F32))
        for d in range(tp):
            both = jnp.concatenate([p[d * OWN : (d + 1) * OWN] for p in parts], axis=0)
            qs[d, pl.ds(pl.multiple_of(pair * 16, 16), 16)] = both.astype(BF16)
        return carry

    lax.fori_loop(0, hh // 2, query_pair, 0)
    slab = hh * OWN
    for step in range(1, tp):
        to = lax.rem(me + step, tp)
        copy = remote(qs.at[to], qr.at[me], qa_sem, (step,), to)
        copy.start()
        sends.append(copy)
    qr[me] = qs[me]

    for step in range(1, tp):
        source = lax.rem(me + tp - step, tp)
        remote(ks.at[source], kr.at[source], ka_sem, (step,), source).wait_recv()
    share = max(1, KEEP // entries)
    fresh = []
    for col in range(KVCB):
        if share == 1:
            total = kr[col // cols, pl.ds((col % cols) * OWN, OWN)]
        else:
            total = kr[col * share]
            for extra in range(1, share):
                total = total + kr[col * share + extra]
        if col < KVH:
            total = total * cos_own + pltpu.roll(total, HD // 2, 1) * sin_own
        fresh.append(total)
    fresh = jnp.concatenate(fresh, axis=1).astype(BF16)
    for r in range(ROW_DEV):
        new_kv[r] = fresh.astype(F32)[r * NEW : (r + 1) * NEW].astype(BF16)
    tail = jnp.concatenate(
        [fresh.astype(F32), jnp.zeros((PAD - OWN, 2 * KVH * HD), F32)], axis=0
    ).astype(BF16)
    for r in range(ROW_DEV):
        kbuf[r, pl.ds(cache_len, PAD)] = tail[:, : KVH * HD]
        vbuf[r, pl.ds(cache_len, PAD)] = tail[:, KVH * HD :]

    for step in range(1, tp):
        source = lax.rem(me + tp - step, tp)
        remote(qs.at[source], qr.at[source], qa_sem, (step,), source).wait_recv()
    for s in range(tp):
        raw = qr[s].astype(F32)
        swapped = pltpu.roll(raw, HD // 2, 1)
        turned = raw.reshape(hh, OWN, HD) * cos_own[None] + swapped.reshape(hh, OWN, HD) * sin_own[None]
        qf[pl.ds(s * slab, slab)] = turned.reshape(slab, HD)
    for copy in k_copies + v_copies:
        copy.wait()

    width = cache_len + PAD
    scale = HD ** (-0.5)
    spot = lax.broadcasted_iota(jnp.int32, (NEW * GROUP, width), 1)
    token = lax.broadcasted_iota(jnp.int32, (NEW * GROUP, width), 0) // GROUP

    def attend_row(r, carry):
        first = cache_len + NEW * r
        valid = (spot < lengths[r]) | ((spot >= first) & (spot <= first + token))
        for g in range(KVH):
            q = jnp.concatenate(
                [qf[pl.ds(g * GROUP * OWN + NEW * r + j, GROUP, stride=OWN)] for j in range(NEW)],
                axis=0,
            ).astype(BF16)
            keys = kbuf[r, :, g * HD : (g + 1) * HD]
            scores = lax.dot_general(
                q, keys, (((1,), (1,)), ((), ())), preferred_element_type=F32
            )
            scores = jnp.where(valid, scores * scale, -1e30)
            top = jnp.max(scores, axis=-1, keepdims=True)
            weights = jnp.where(valid, jnp.exp(scores - top), 0.0).astype(BF16)
            below = jnp.sum(weights.astype(F32), axis=-1, keepdims=True)
            values = vbuf[r, :, g * HD : (g + 1) * HD]
            above = jnp.dot(weights, values, preferred_element_type=F32)
            result = above / below
            for j in range(NEW):
                af[pl.ds(g * GROUP * OWN + NEW * r + j, GROUP, stride=OWN)] = result[
                    j * GROUP : (j + 1) * GROUP
                ]
        return carry

    lax.fori_loop(0, ROW_DEV, attend_row, 0)

    for d in range(tp):
        asend[d] = af[pl.ds(d * slab, slab)].astype(BF16)
    for step in range(1, tp):
        to = lax.rem(me + step, tp)
        copy = remote(asend.at[to], ar.at[me], aa_sem, (step,), to)
        copy.start()
        sends.append(copy)
    ar[me] = asend[me]
    for copy in o_copies:
        copy.wait()
    for step in range(1, tp):
        source = lax.rem(me + tp - step, tp)
        remote(asend.at[source], ar.at[source], aa_sem, (step,), source).wait_recv()

    order = [y * 2 + c for c in range(2) for y in range(ny)]
    heads = [ar[s].astype(F32) for s in order]
    for i in range(hh):
        lhs = jnp.concatenate([h[i * OWN : (i + 1) * OWN] for h in heads], axis=0)
        xo[:, i * BLK : (i + 1) * BLK] = lhs.astype(BF16)

    pairs = DB // CHUNKS // 2
    side = ny * OWN

    def stage1(ch):
        return remote(pbuf.at[ch, 1 - mc], rbuf.at[ch], s1_sem, (ch,), other)

    def stage2(ch, step):
        to = lax.rem(my + step, ny)
        piece = sbuf.at[ch, pl.ds(pl.multiple_of(to * OWN, OWN), OWN)]
        return remote(piece, fbuf.at[ch, my], s2_sem, (ch, step), to * 2 + mc)

    def pass_on(ch):
        stage1(ch).wait_recv()
        sbuf[ch] = pbuf[ch, mc] + rbuf[ch]
        for step in range(1, ny):
            stage2(ch, step).start()

    def project(ch, carry):
        def one_pair(pair, inner):
            n = (ch * pairs + pair) * 2
            total = None
            ahead = [reached[i] for i in range(hh)]
            slots = []
            for a in range(2):
                for i in range(hh):
                    at = ahead[i]
                    hit = o_cols[i, jnp.minimum(at, KEEP - 1)] == n + a
                    slots.append(jnp.where(hit, i * KEEP + at, hh * KEEP))
                    ahead[i] = at + hit.astype(jnp.int32)
            wide_k = 2 if hh % 2 == 0 else 1
            for i in range(0, hh, wide_k):
                w = jnp.concatenate(
                    [
                        jnp.concatenate(
                            [wo[slots[a * hh + i + b]] for b in range(wide_k)], axis=0
                        )
                        for a in range(2)
                    ],
                    axis=1,
                )
                part = jnp.dot(
                    xo[:, i * BLK : (i + wide_k) * BLK], w, preferred_element_type=F32
                )
                total = part if total is None else total + part
            columns = pl.ds(pl.multiple_of(pair * 2 * BLK, 2 * BLK), 2 * BLK)
            for c in range(2):
                pbuf[ch, c, :, columns] = total[c * side : (c + 1) * side]
            for i in range(hh):
                reached[i] = ahead[i]
            return inner

        lax.fori_loop(0, pairs, one_pair, 0)
        stage1(ch).start()

        @pl.when(ch > 0)
        def _():
            pass_on(ch - 1)

        return carry

    for i in range(hh):
        reached[i] = 0
    lax.fori_loop(0, CHUNKS, project, 0)
    pass_on(CHUNKS - 1)

    def finish(ch, carry):
        total = sbuf[ch, pl.ds(pl.multiple_of(my * OWN, OWN), OWN)]
        for step in range(1, ny):
            source = lax.rem(my + ny - step, ny)
            remote(
                sbuf.at[ch, pl.ds(0, OWN)], fbuf.at[ch, source], s2_sem, (ch, step), other
            ).wait_recv()
            total = total + fbuf[ch, source]
        wide_chunk = D // CHUNKS
        columns = pl.ds(pl.multiple_of(ch * wide_chunk, wide_chunk), wide_chunk)
        for r in range(ROW_DEV):
            out[r, :, columns] = total[r * NEW : (r + 1) * NEW].astype(BF16)
        return carry

    lax.fori_loop(0, CHUNKS, finish, 0)

    x1.wait_send()
    for copy in x2 + x3 + sends:
        copy.wait_send()

    def drain(ch, carry):
        stage1(ch).wait_send()
        for step in range(1, ny):
            stage2(ch, step).wait_send()
        return carry

    lax.fori_loop(0, CHUNKS, drain, 0)


def on_device(
    tp,
    hidden_states,
    norm_gain,
    q_blocks,
    q_rows,
    kv_blocks,
    kv_rows,
    o_blocks,
    o_cols,
    key_cache,
    value_cache,
    lengths,
):
    hh = q_blocks.shape[0]
    entries = kv_blocks.shape[0]
    cache_len = key_cache.shape[1]
    ny = tp // 2
    vmem = pl.BlockSpec(memory_space=pltpu.VMEM)
    smem = pl.BlockSpec(memory_space=pltpu.SMEM)
    anywhere = pl.BlockSpec(memory_space=pl.ANY)
    slab = hh * OWN
    cols = max(1, entries // KEEP)
    width = cache_len + PAD
    chunk = D // CHUNKS
    dma = pltpu.SemaphoreType.DMA
    return pl.pallas_call(
        functools.partial(kernel, tp, hh, entries, cache_len),
        out_shape=(
            jax.ShapeDtypeStruct((ROW_DEV, NEW, D), BF16),
            jax.ShapeDtypeStruct((ROW_DEV, NEW, 2 * KVH * HD), BF16),
        ),
        in_specs=[vmem] * 2 + [smem] * 4 + [anywhere] * 5,
        out_specs=(vmem, vmem),
        scratch_shapes=[
            pltpu.VMEM((hh, KEEP, BLK, BLK), BF16),
            pltpu.VMEM((entries, BLK, BLK), BF16),
            pltpu.VMEM((hh * KEEP + 1, BLK, BLK), BF16),
            pltpu.VMEM((ROW_DEV, width, KVH * HD), BF16),
            pltpu.VMEM((ROW_DEV, width, KVH * HD), BF16),
            pltpu.VMEM((2, DB, OWN, BLK), F32),
            pltpu.VMEM((ny, DB, 2 * OWN, BLK), BF16),
            pltpu.VMEM((tp, slab, HD), BF16),
            pltpu.VMEM((tp, slab, HD), BF16),
            pltpu.VMEM((tp * slab, HD), F32),
            pltpu.VMEM((tp, cols * OWN, BLK), F32),
            pltpu.VMEM((tp, cols * OWN, BLK), F32),
            pltpu.VMEM((tp * slab, HD), F32),
            pltpu.VMEM((tp, slab, HD), BF16),
            pltpu.VMEM((tp, slab, HD), BF16),
            pltpu.VMEM((tp * OWN, hh * BLK), BF16),
            pltpu.VMEM((CHUNKS, 2, ny * OWN, chunk), F32),
            pltpu.VMEM((CHUNKS, ny * OWN, chunk), F32),
            pltpu.VMEM((CHUNKS, ny * OWN, chunk), F32),
            pltpu.VMEM((CHUNKS, ny, OWN, chunk), F32),
            pltpu.SMEM((hh,), jnp.int32),
            dma((hh,)),
            dma,
            dma((hh,)),
            dma((2, ROW_DEV)),
            dma((2, 1)),
            dma((2, ny)),
            dma((2, ny)),
            dma((2, tp)),
            dma((2, tp)),
            dma((2, tp)),
            dma((2, CHUNKS)),
            dma((2, CHUNKS, ny)),
        ],
        compiler_params=pltpu.CompilerParams(
            collective_id=0, has_side_effects=True, vmem_limit_bytes=60 * 1024 * 1024
        ),
    )(
        hidden_states,
        norm_gain,
        q_rows,
        kv_rows,
        o_cols,
        lengths,
        q_blocks,
        kv_blocks,
        o_blocks,
        key_cache,
        value_cache,
    )


def solution(mesh):
    rows = P(("groups", "tensor", "dp"), None, None)
    return jax.shard_map(
        functools.partial(on_device, mesh.shape["tensor"]),
        mesh=mesh,
        in_specs=(
            rows,
            P(),
            P("tensor", None, None, None),
            P("tensor", None),
            P("tensor", None, None),
            P("tensor"),
            P("tensor", None, None, None),
            P("tensor", None),
            rows,
            rows,
            P(("groups", "tensor", "dp")),
        ),
        out_specs=(rows, rows),
        check_vma=False,
    )
```

```python
import functools
import math

import jax
import jax.numpy as jnp
from jax import lax
from jax.experimental import pallas as pl
from jax.experimental.pallas import tpu as pltpu
from jax.sharding import PartitionSpec as P

D = 8192
BLK = 128
QH = 64
KVH = 4
HD = 128
NEW = 2
DB = 64
KEEP = 32
KVCB = 8
ROW_DEV = 4
OWN = ROW_DEV * NEW
GROUP = QH // KVH
PAD = 128
CHUNKS = 8
PIECES = 2
UO = 4
UA = 4
UQ = 4
MESH = pl.DeviceIdType.MESH
F32 = jnp.float32
BF16 = jnp.bfloat16


def kernel(
    tp,
    hh,
    entries,
    cache_len,
    lengths,
    hidden_hbm,
    gain_hbm,
    q_rows_hbm,
    kv_rows_hbm,
    o_cols_hbm,
    q_hbm,
    kv_hbm,
    o_hbm,
    k_hbm,
    v_hbm,
    out,
    new_kv,
    wq,
    wkv,
    wo,
    kbuf,
    vbuf,
    xs,
    xg,
    qs,
    qr,
    qf,
    ks,
    kr,
    af,
    asend,
    ar,
    xo,
    pbuf,
    rbuf,
    sbuf,
    fbuf,
    reached,
    hidden,
    gain,
    q_rows,
    kv_rows,
    o_cols,
    in_sem,
    q_sem,
    kv_sem,
    o_sem,
    c_sem,
    x1_sem,
    x2_sem,
    x3_sem,
    qa_sem,
    ka_sem,
    aa_sem,
    s1_sem,
    s2_sem,
):
    ny = tp // 2
    me = lax.axis_index("tensor")
    my = me // 2
    mc = lax.rem(me, 2)
    other = my * 2 + (1 - mc)

    barrier = pltpu.get_barrier_semaphore()
    for step in range(1, tp):
        pl.semaphore_signal(
            barrier, inc=1, device_id={"tensor": lax.rem(me + step, tp)}, device_id_type=MESH
        )

    fetched = (
        (hidden_hbm, hidden),
        (gain_hbm, gain),
        (q_rows_hbm, q_rows),
        (kv_rows_hbm, kv_rows),
        (o_cols_hbm, o_cols),
    )
    in_copies = [pltpu.make_async_copy(a, b, in_sem.at[i]) for i, (a, b) in enumerate(fetched)]
    for copy in in_copies:
        copy.start()
    q_copies = [pltpu.make_async_copy(q_hbm.at[c], wq.at[c], q_sem.at[c]) for c in range(hh)]
    kv_copy = pltpu.make_async_copy(kv_hbm, wkv, kv_sem)
    k_copies = [
        pltpu.make_async_copy(k_hbm.at[r], kbuf.at[r, pl.ds(0, cache_len)], c_sem.at[0, r])
        for r in range(ROW_DEV)
    ]
    v_copies = [
        pltpu.make_async_copy(v_hbm.at[r], vbuf.at[r, pl.ds(0, cache_len)], c_sem.at[1, r])
        for r in range(ROW_DEV)
    ]
    o_copies = [
        pltpu.make_async_copy(o_hbm.at[i], wo.at[pl.ds(i * KEEP, KEEP)], o_sem.at[i])
        for i in range(hh)
    ]
    kv_copy.start()
    for copy in q_copies:
        copy.start()

    def remote(src, dst, sems, slot, target):
        return pltpu.make_async_remote_copy(
            src_ref=src,
            dst_ref=dst,
            send_sem=sems.at[(0,) + slot],
            recv_sem=sems.at[(1,) + slot],
            device_id={"tensor": target},
            device_id_type=MESH,
        )

    for copy in in_copies:
        copy.wait()
    wide = jnp.concatenate([hidden[r].astype(F32) for r in range(ROW_DEV)], axis=0)
    inv_rms = lax.rsqrt(jnp.mean(wide * wide, axis=-1, keepdims=True) + 1e-05)
    normed = (wide * inv_rms * gain[...].astype(F32).reshape(1, D)).astype(BF16).astype(F32)
    for b in range(0, DB, 2):
        both = [normed[:, n * BLK : (n + 1) * BLK] for n in (b, b + 1)]
        xs[me, b * OWN : (b + 2) * OWN] = jnp.concatenate(both, axis=0).astype(BF16)
    wo[hh * KEEP] = jnp.zeros((BLK, BLK), BF16)

    lane = lax.broadcasted_iota(jnp.int32, (OWN, HD), 1)
    row = lax.broadcasted_iota(jnp.int32, (OWN, HD), 0)
    position = lax.rem(row, NEW)
    for r in range(ROW_DEV):
        position = position + jnp.where(row // NEW == r, lengths[r], 0)
    exponent = lax.rem(lane, HD // 2).astype(F32) * (-math.log(500000.0) / (HD // 2))
    angles = position.astype(F32) * jnp.exp(exponent)
    cos_own = jnp.cos(angles)
    sin_own = jnp.sin(angles)
    sin_own = jnp.where(lane < HD // 2, -sin_own, sin_own)

    pl.semaphore_wait(barrier, tp - 1)

    piece_rows = DB * OWN // PIECES
    pieces = [pl.ds(p * piece_rows, piece_rows) for p in range(PIECES)]
    x2 = []
    for p in range(PIECES):
        for step in range(1, ny):
            to = lax.rem(my + step, ny)
            part = xs.at[me, pieces[p]]
            copy = remote(part, part, x2_sem, (step, p), to * 2 + mc)
            copy.start()
            x2.append(copy)
    x1 = remote(xs.at[me], xs.at[me], x1_sem, (0,), other)
    x1.start()
    for copy in k_copies + v_copies:
        copy.start()

    def assemble(y):
        sides = [xs[y * 2 + c].astype(F32).reshape(DB, OWN, BLK) for c in range(2)]
        xg[y] = jnp.concatenate(sides, axis=1).astype(BF16)

    remote(xs.at[other], xs.at[other], x1_sem, (0,), other).wait_recv()
    assemble(my)

    x3 = []
    for p in range(PIECES):
        for step in range(1, ny):
            source = lax.rem(my + ny - step, ny)
            part = xs.at[source * 2 + mc, pieces[p]]
            remote(part, part, x2_sem, (step, p), other).wait_recv()
            copy = remote(part, part, x3_sem, (step, p), other)
            copy.start()
            x3.append(copy)
    for step in range(1, ny):
        source = lax.rem(my + ny - step, ny)
        for p in range(PIECES):
            part = xs.at[source * 2 + 1 - mc, pieces[p]]
            remote(part, part, x3_sem, (step, p), other).wait_recv()
        assemble(source)

    def picked(rows):
        blocks = [jnp.concatenate([xg[y, row] for y in range(ny)], axis=0) for row in rows]
        return jnp.concatenate(blocks, axis=1)

    kv_copy.wait()
    cols = max(1, entries // KEEP)
    per = entries // cols
    for col in range(cols):
        x = picked([kv_rows[col * per + e] for e in range(per)])
        w = wkv[pl.ds(col * per, per)].reshape(per * BLK, BLK)
        part = jnp.dot(x, w, preferred_element_type=F32)
        for d in range(tp):
            ks[d, pl.ds(col * OWN, OWN)] = part[d * OWN : (d + 1) * OWN]
    sends = []
    for step in range(1, tp):
        to = lax.rem(me + step, tp)
        copy = remote(ks.at[to], kr.at[me], ka_sem, (step,), to)
        copy.start()
        sends.append(copy)
    kr[me] = ks[me]

    for copy in q_copies:
        copy.wait()
    for copy in o_copies:
        copy.start()

    def query_pair(pair, carry):
        parts = []
        for s in range(2):
            c = pair * 2 + s
            x = picked([q_rows[c, k] for k in range(KEEP)])
            w = wq[c].reshape(KEEP * BLK, BLK)
            parts.append(jnp.dot(x, w, preferred_element_type=F32))
        for d in range(tp):
            both = jnp.concatenate([p[d * OWN : (d + 1) * OWN] for p in parts], axis=0)
            qs[d, pl.ds(pl.multiple_of(pair * 16, 16), 16)] = both.astype(BF16)
        return carry

    lax.fori_loop(0, hh // 2, query_pair, 0, unroll=UQ)
    slab = hh * OWN
    for step in range(1, tp):
        to = lax.rem(me + step, tp)
        copy = remote(qs.at[to], qr.at[me], qa_sem, (step,), to)
        copy.start()
        sends.append(copy)
    qr[me] = qs[me]

    for step in range(1, tp):
        source = lax.rem(me + tp - step, tp)
        remote(ks.at[source], kr.at[source], ka_sem, (step,), source).wait_recv()
    share = max(1, KEEP // entries)
    fresh = []
    for col in range(KVCB):
        if share == 1:
            total = kr[col // cols, pl.ds((col % cols) * OWN, OWN)]
        else:
            total = kr[col * share]
            for extra in range(1, share):
                total = total + kr[col * share + extra]
        if col < KVH:
            total = total * cos_own + pltpu.roll(total, HD // 2, 1) * sin_own
        fresh.append(total)
    fresh = jnp.concatenate(fresh, axis=1).astype(BF16)
    for r in range(ROW_DEV):
        new_kv[r] = fresh.astype(F32)[r * NEW : (r + 1) * NEW].astype(BF16)
    tail = jnp.concatenate(
        [fresh.astype(F32), jnp.zeros((PAD - OWN, 2 * KVH * HD), F32)], axis=0
    ).astype(BF16)
    for r in range(ROW_DEV):
        kbuf[r, pl.ds(cache_len, PAD)] = tail[:, : KVH * HD]
        vbuf[r, pl.ds(cache_len, PAD)] = tail[:, KVH * HD :]

    for step in range(1, tp):
        source = lax.rem(me + tp - step, tp)
        remote(qs.at[source], qr.at[source], qa_sem, (step,), source).wait_recv()
    for s in range(tp):
        raw = qr[s].astype(F32)
        swapped = pltpu.roll(raw, HD // 2, 1)
        turned = raw.reshape(hh, OWN, HD) * cos_own[None] + swapped.reshape(hh, OWN, HD) * sin_own[None]
        qf[pl.ds(s * slab, slab)] = turned.reshape(slab, HD)
    for copy in k_copies + v_copies:
        copy.wait()

    width = cache_len + PAD
    scale = HD ** (-0.5)
    spot = lax.broadcasted_iota(jnp.int32, (NEW * GROUP, width), 1)
    token = lax.broadcasted_iota(jnp.int32, (NEW * GROUP, width), 0) // GROUP

    def attend_row(r, carry):
        first = cache_len + NEW * r
        valid = (spot < lengths[r]) | ((spot >= first) & (spot <= first + token))
        for g in range(KVH):
            q = jnp.concatenate(
                [qf[pl.ds(g * GROUP * OWN + NEW * r + j, GROUP, stride=OWN)] for j in range(NEW)],
                axis=0,
            ).astype(BF16)
            keys = kbuf[r, :, g * HD : (g + 1) * HD]
            scores = lax.dot_general(
                q, keys, (((1,), (1,)), ((), ())), preferred_element_type=F32
            )
            scores = jnp.where(valid, scores * scale, -1e30)
            top = jnp.max(scores, axis=-1, keepdims=True)
            weights = jnp.where(valid, jnp.exp(scores - top), 0.0).astype(BF16)
            below = jnp.sum(weights.astype(F32), axis=-1, keepdims=True)
            values = vbuf[r, :, g * HD : (g + 1) * HD]
            above = jnp.dot(weights, values, preferred_element_type=F32)
            result = above / below
            for j in range(NEW):
                af[pl.ds(g * GROUP * OWN + NEW * r + j, GROUP, stride=OWN)] = result[
                    j * GROUP : (j + 1) * GROUP
                ]
        return carry

    lax.fori_loop(0, ROW_DEV, attend_row, 0, unroll=UA)

    for d in range(tp):
        asend[d] = af[pl.ds(d * slab, slab)].astype(BF16)
    for step in range(1, tp):
        to = lax.rem(me + step, tp)
        copy = remote(asend.at[to], ar.at[me], aa_sem, (step,), to)
        copy.start()
        sends.append(copy)
    ar[me] = asend[me]
    for copy in o_copies:
        copy.wait()
    for step in range(1, tp):
        source = lax.rem(me + tp - step, tp)
        remote(asend.at[source], ar.at[source], aa_sem, (step,), source).wait_recv()

    order = [y * 2 + c for c in range(2) for y in range(ny)]
    heads = [ar[s].astype(F32) for s in order]
    for i in range(hh):
        lhs = jnp.concatenate([h[i * OWN : (i + 1) * OWN] for h in heads], axis=0)
        xo[:, i * BLK : (i + 1) * BLK] = lhs.astype(BF16)

    pairs = DB // CHUNKS // 2
    side = ny * OWN

    def stage1(ch):
        return remote(pbuf.at[ch, 1 - mc], rbuf.at[ch], s1_sem, (ch,), other)

    def stage2(ch, step):
        to = lax.rem(my + step, ny)
        piece = sbuf.at[ch, pl.ds(pl.multiple_of(to * OWN, OWN), OWN)]
        return remote(piece, fbuf.at[ch, my], s2_sem, (ch, step), to * 2 + mc)

    def pass_on(ch):
        stage1(ch).wait_recv()
        sbuf[ch] = pbuf[ch, mc] + rbuf[ch]
        for step in range(1, ny):
            stage2(ch, step).start()

    def project(ch, carry):
        def one_pair(pair, inner):
            n = (ch * pairs + pair) * 2
            total = None
            ahead = [reached[i] for i in range(hh)]
            slots = []
            for a in range(2):
                for i in range(hh):
                    at = ahead[i]
                    hit = o_cols[i, jnp.minimum(at, KEEP - 1)] == n + a
                    slots.append(jnp.where(hit, i * KEEP + at, hh * KEEP))
                    ahead[i] = at + hit.astype(jnp.int32)
            wide_k = 2 if hh % 2 == 0 else 1
            for i in range(0, hh, wide_k):
                w = jnp.concatenate(
                    [
                        jnp.concatenate(
                            [wo[slots[a * hh + i + b]] for b in range(wide_k)], axis=0
                        )
                        for a in range(2)
                    ],
                    axis=1,
                )
                part = jnp.dot(
                    xo[:, i * BLK : (i + wide_k) * BLK], w, preferred_element_type=F32
                )
                total = part if total is None else total + part
            columns = pl.ds(pl.multiple_of(pair * 2 * BLK, 2 * BLK), 2 * BLK)
            for c in range(2):
                pbuf[ch, c, :, columns] = total[c * side : (c + 1) * side]
            for i in range(hh):
                reached[i] = ahead[i]
            return inner

        lax.fori_loop(0, pairs, one_pair, 0, unroll=UO)
        stage1(ch).start()

        @pl.when(ch > 0)
        def _():
            pass_on(ch - 1)

        return carry

    for i in range(hh):
        reached[i] = 0
    lax.fori_loop(0, CHUNKS, project, 0)
    pass_on(CHUNKS - 1)

    def finish(ch, carry):
        total = sbuf[ch, pl.ds(pl.multiple_of(my * OWN, OWN), OWN)]
        for step in range(1, ny):
            source = lax.rem(my + ny - step, ny)
            remote(
                sbuf.at[ch, pl.ds(0, OWN)], fbuf.at[ch, source], s2_sem, (ch, step), other
            ).wait_recv()
            total = total + fbuf[ch, source]
        wide_chunk = D // CHUNKS
        columns = pl.ds(pl.multiple_of(ch * wide_chunk, wide_chunk), wide_chunk)
        for r in range(ROW_DEV):
            out[r, :, columns] = total[r * NEW : (r + 1) * NEW].astype(BF16)
        return carry

    lax.fori_loop(0, CHUNKS, finish, 0)

    x1.wait_send()
    for copy in x2 + x3 + sends:
        copy.wait_send()

    def drain(ch, carry):
        stage1(ch).wait_send()
        for step in range(1, ny):
            stage2(ch, step).wait_send()
        return carry

    lax.fori_loop(0, CHUNKS, drain, 0)


def on_device(
    tp,
    hidden_states,
    norm_gain,
    q_blocks,
    q_rows,
    kv_blocks,
    kv_rows,
    o_blocks,
    o_cols,
    key_cache,
    value_cache,
    lengths,
):
    hh = q_blocks.shape[0]
    entries = kv_blocks.shape[0]
    cache_len = key_cache.shape[1]
    ny = tp // 2
    vmem = pl.BlockSpec(memory_space=pltpu.VMEM)
    smem = pl.BlockSpec(memory_space=pltpu.SMEM)
    hbm = pl.BlockSpec(memory_space=pltpu.HBM)
    slab = hh * OWN
    cols = max(1, entries // KEEP)
    width = cache_len + PAD
    chunk = D // CHUNKS
    dma = pltpu.SemaphoreType.DMA
    return pl.pallas_call(
        functools.partial(kernel, tp, hh, entries, cache_len),
        out_shape=(
            jax.ShapeDtypeStruct((ROW_DEV, NEW, D), BF16),
            jax.ShapeDtypeStruct((ROW_DEV, NEW, 2 * KVH * HD), BF16),
        ),
        in_specs=[smem] + [hbm] * 10,
        out_specs=(vmem, vmem),
        scratch_shapes=[
            pltpu.VMEM((hh, KEEP, BLK, BLK), BF16),
            pltpu.VMEM((entries, BLK, BLK), BF16),
            pltpu.VMEM((hh * KEEP + 1, BLK, BLK), BF16),
            pltpu.VMEM((ROW_DEV, width, KVH * HD), BF16),
            pltpu.VMEM((ROW_DEV, width, KVH * HD), BF16),
            pltpu.VMEM((tp, DB * OWN, BLK), BF16),
            pltpu.VMEM((ny, DB, 2 * OWN, BLK), BF16),
            pltpu.VMEM((tp, slab, HD), BF16),
            pltpu.VMEM((tp, slab, HD), BF16),
            pltpu.VMEM((tp * slab, HD), F32),
            pltpu.VMEM((tp, cols * OWN, BLK), F32),
            pltpu.VMEM((tp, cols * OWN, BLK), F32),
            pltpu.VMEM((tp * slab, HD), F32),
            pltpu.VMEM((tp, slab, HD), BF16),
            pltpu.VMEM((tp, slab, HD), BF16),
            pltpu.VMEM((tp * OWN, hh * BLK), BF16),
            pltpu.VMEM((CHUNKS, 2, ny * OWN, chunk), F32),
            pltpu.VMEM((CHUNKS, ny * OWN, chunk), F32),
            pltpu.VMEM((CHUNKS, ny * OWN, chunk), F32),
            pltpu.VMEM((CHUNKS, ny, OWN, chunk), F32),
            pltpu.SMEM((hh,), jnp.int32),
            pltpu.VMEM((ROW_DEV, NEW, D), BF16),
            pltpu.VMEM((D,), BF16),
            pltpu.SMEM((hh, KEEP), jnp.int32),
            pltpu.SMEM((entries,), jnp.int32),
            pltpu.SMEM((hh, KEEP), jnp.int32),
            dma((5,)),
            dma((hh,)),
            dma,
            dma((hh,)),
            dma((2, ROW_DEV)),
            dma((2, 1)),
            dma((2, ny, PIECES)),
            dma((2, ny, PIECES)),
            dma((2, tp)),
            dma((2, tp)),
            dma((2, tp)),
            dma((2, CHUNKS)),
            dma((2, CHUNKS, ny)),
        ],
        compiler_params=pltpu.CompilerParams(
            collective_id=0, has_side_effects=True, vmem_limit_bytes=60 * 1024 * 1024
        ),
    )(
        lengths,
        hidden_states,
        norm_gain,
        q_rows,
        kv_rows,
        o_cols,
        q_blocks,
        kv_blocks,
        o_blocks,
        key_cache,
        value_cache,
    )


def solution(mesh):
    rows = P(("groups", "tensor", "dp"), None, None)
    return jax.shard_map(
        functools.partial(on_device, mesh.shape["tensor"]),
        mesh=mesh,
        in_specs=(
            rows,
            P(),
            P("tensor", None, None, None),
            P("tensor", None),
            P("tensor", None, None),
            P("tensor"),
            P("tensor", None, None, None),
            P("tensor", None),
            rows,
            rows,
            P(("groups", "tensor", "dp")),
        ),
        out_specs=(rows, rows),
        check_vma=False,
    )
```

```python
import functools
import math

import jax
import jax.numpy as jnp
from jax import lax
from jax.experimental import pallas as pl
from jax.experimental.pallas import tpu as pltpu
from jax.sharding import PartitionSpec as P

D = 8192
BLK = 128
QH = 64
KVH = 4
HD = 128
NEW = 2
DB = 64
KEEP = 32
KVCB = 8
ROW_DEV = 4
OWN = ROW_DEV * NEW
GROUP = QH // KVH
PAD = 128
CHUNKS = 8
PIECES = 2
UO = 4
UA = 4
UQ = 4
MESH = pl.DeviceIdType.MESH
F32 = jnp.float32
BF16 = jnp.bfloat16


def kernel(
    tp,
    hh,
    entries,
    cache_len,
    lengths,
    hidden_hbm,
    gain_hbm,
    q_rows_hbm,
    kv_rows_hbm,
    o_cols_hbm,
    q_hbm,
    kv_hbm,
    o_hbm,
    k_hbm,
    v_hbm,
    out,
    new_kv,
    wq,
    wkv,
    wo,
    kbuf,
    vbuf,
    xs,
    xg,
    qs,
    qr,
    qf,
    ks,
    kr,
    af,
    asend,
    ar,
    xo,
    pbuf,
    rbuf,
    sbuf,
    fbuf,
    reached,
    hidden,
    gain,
    q_rows,
    kv_rows,
    o_cols,
    in_sem,
    q_sem,
    kv_sem,
    o_sem,
    c_sem,
    x1_sem,
    x2_sem,
    x3_sem,
    qa_sem,
    ka_sem,
    aa_sem,
    s1_sem,
    s2_sem,
):
    ny = tp // 2
    me = lax.axis_index("tensor")
    my = me // 2
    mc = lax.rem(me, 2)
    other = my * 2 + (1 - mc)

    barrier = pltpu.get_barrier_semaphore()
    for step in range(1, tp):
        pl.semaphore_signal(
            barrier, inc=1, device_id={"tensor": lax.rem(me + step, tp)}, device_id_type=MESH
        )

    fetched = (
        (hidden_hbm, hidden),
        (gain_hbm, gain),
        (q_rows_hbm, q_rows),
        (kv_rows_hbm, kv_rows),
        (o_cols_hbm, o_cols),
    )
    in_copies = [pltpu.make_async_copy(a, b, in_sem.at[i]) for i, (a, b) in enumerate(fetched)]
    for copy in in_copies:
        copy.start()
    q_copies = [pltpu.make_async_copy(q_hbm.at[c], wq.at[c], q_sem.at[c]) for c in range(hh)]
    kv_copy = pltpu.make_async_copy(kv_hbm, wkv, kv_sem)
    k_copies = [
        pltpu.make_async_copy(k_hbm.at[r], kbuf.at[r, pl.ds(0, cache_len)], c_sem.at[0, r])
        for r in range(ROW_DEV)
    ]
    v_copies = [
        pltpu.make_async_copy(v_hbm.at[r], vbuf.at[r, pl.ds(0, cache_len)], c_sem.at[1, r])
        for r in range(ROW_DEV)
    ]
    o_copies = [
        pltpu.make_async_copy(o_hbm.at[i], wo.at[pl.ds(i * KEEP, KEEP)], o_sem.at[i])
        for i in range(hh)
    ]
    kv_copy.start()
    for copy in q_copies:
        copy.start()

    def remote(src, dst, sems, slot, target):
        return pltpu.make_async_remote_copy(
            src_ref=src,
            dst_ref=dst,
            send_sem=sems.at[(0,) + slot],
            recv_sem=sems.at[(1,) + slot],
            device_id={"tensor": target},
            device_id_type=MESH,
        )

    for copy in in_copies:
        copy.wait()
    wide = jnp.concatenate([hidden[r].astype(F32) for r in range(ROW_DEV)], axis=0)
    inv_rms = lax.rsqrt(jnp.mean(wide * wide, axis=-1, keepdims=True) + 1e-05)
    normed = (wide * inv_rms * gain[...].astype(F32).reshape(1, D)).astype(BF16).astype(F32)
    for b in range(0, DB, 2):
        both = [normed[:, n * BLK : (n + 1) * BLK] for n in (b, b + 1)]
        xs[me, b * OWN : (b + 2) * OWN] = jnp.concatenate(both, axis=0).astype(BF16)
    wo[hh * KEEP] = jnp.zeros((BLK, BLK), BF16)

    lane = lax.broadcasted_iota(jnp.int32, (OWN, HD), 1)
    row = lax.broadcasted_iota(jnp.int32, (OWN, HD), 0)
    position = lax.rem(row, NEW)
    for r in range(ROW_DEV):
        position = position + jnp.where(row // NEW == r, lengths[r], 0)
    exponent = lax.rem(lane, HD // 2).astype(F32) * (-math.log(500000.0) / (HD // 2))
    angles = position.astype(F32) * jnp.exp(exponent)
    cos_own = jnp.cos(angles)
    sin_own = jnp.sin(angles)
    sin_own = jnp.where(lane < HD // 2, -sin_own, sin_own)

    pl.semaphore_wait(barrier, tp - 1)

    piece_rows = DB * OWN // PIECES
    pieces = [pl.ds(p * piece_rows, piece_rows) for p in range(PIECES)]
    x2 = []
    for p in range(PIECES):
        for step in range(1, ny):
            to = lax.rem(my + step, ny)
            part = xs.at[me, pieces[p]]
            copy = remote(part, part, x2_sem, (step, p), to * 2 + mc)
            copy.start()
            x2.append(copy)
    x1 = remote(xs.at[me], xs.at[me], x1_sem, (0,), other)
    x1.start()
    for copy in k_copies + v_copies:
        copy.start()

    def assemble(y):
        sides = [xs[y * 2 + c].astype(F32).reshape(DB, OWN, BLK) for c in range(2)]
        xg[y] = jnp.concatenate(sides, axis=1).astype(BF16)

    remote(xs.at[other], xs.at[other], x1_sem, (0,), other).wait_recv()
    assemble(my)

    x3 = []
    for p in range(PIECES):
        for step in range(1, ny):
            source = lax.rem(my + ny - step, ny)
            part = xs.at[source * 2 + mc, pieces[p]]
            remote(part, part, x2_sem, (step, p), other).wait_recv()
            copy = remote(part, part, x3_sem, (step, p), other)
            copy.start()
            x3.append(copy)
    for step in range(1, ny):
        source = lax.rem(my + ny - step, ny)
        for p in range(PIECES):
            part = xs.at[source * 2 + 1 - mc, pieces[p]]
            remote(part, part, x3_sem, (step, p), other).wait_recv()
        assemble(source)

    def picked(rows):
        blocks = [jnp.concatenate([xg[y, row] for y in range(ny)], axis=0) for row in rows]
        return jnp.concatenate(blocks, axis=1)

    kv_copy.wait()
    cols = max(1, entries // KEEP)
    per = entries // cols
    for col in range(cols):
        x = picked([kv_rows[col * per + e] for e in range(per)])
        w = wkv[pl.ds(col * per, per)].reshape(per * BLK, BLK)
        part = jnp.dot(x, w, preferred_element_type=F32)
        for d in range(tp):
            ks[d, pl.ds(col * OWN, OWN)] = part[d * OWN : (d + 1) * OWN]
    sends = []
    for step in range(1, tp):
        to = lax.rem(me + step, tp)
        copy = remote(ks.at[to], kr.at[me], ka_sem, (step,), to)
        copy.start()
        sends.append(copy)
    kr[me] = ks[me]

    for copy in q_copies:
        copy.wait()
    for copy in o_copies:
        copy.start()

    def query_pair(pair, carry):
        parts = []
        for s in range(2):
            c = pair * 2 + s
            x = picked([q_rows[c, k] for k in range(KEEP)])
            w = wq[c].reshape(KEEP * BLK, BLK)
            parts.append(jnp.dot(x, w, preferred_element_type=F32))
        for d in range(tp):
            both = jnp.concatenate([p[d * OWN : (d + 1) * OWN] for p in parts], axis=0)
            qs[d, pl.ds(pl.multiple_of(pair * 16, 16), 16)] = both.astype(BF16)
        return carry

    lax.fori_loop(0, hh // 2, query_pair, 0, unroll=UQ)
    slab = hh * OWN
    for step in range(1, tp):
        to = lax.rem(me + step, tp)
        copy = remote(qs.at[to], qr.at[me], qa_sem, (step,), to)
        copy.start()
        sends.append(copy)
    qr[me] = qs[me]

    for step in range(1, tp):
        source = lax.rem(me + tp - step, tp)
        remote(ks.at[source], kr.at[source], ka_sem, (step,), source).wait_recv()
    share = max(1, KEEP // entries)
    fresh = []
    for col in range(KVCB):
        if share == 1:
            total = kr[col // cols, pl.ds((col % cols) * OWN, OWN)]
        else:
            total = kr[col * share]
            for extra in range(1, share):
                total = total + kr[col * share + extra]
        if col < KVH:
            total = total * cos_own + pltpu.roll(total, HD // 2, 1) * sin_own
        fresh.append(total)
    fresh = jnp.concatenate(fresh, axis=1).astype(BF16)
    for r in range(ROW_DEV):
        new_kv[r] = fresh.astype(F32)[r * NEW : (r + 1) * NEW].astype(BF16)
    tail = jnp.concatenate(
        [fresh.astype(F32), jnp.zeros((PAD - OWN, 2 * KVH * HD), F32)], axis=0
    ).astype(BF16)
    for r in range(ROW_DEV):
        kbuf[r, pl.ds(cache_len, PAD)] = tail[:, : KVH * HD]
        vbuf[r, pl.ds(cache_len, PAD)] = tail[:, KVH * HD :]

    for step in range(1, tp):
        source = lax.rem(me + tp - step, tp)
        remote(qs.at[source], qr.at[source], qa_sem, (step,), source).wait_recv()
    for s in range(tp):
        raw = qr[s].astype(F32)
        swapped = pltpu.roll(raw, HD // 2, 1)
        turned = raw.reshape(hh, OWN, HD) * cos_own[None] + swapped.reshape(hh, OWN, HD) * sin_own[None]
        qf[pl.ds(s * slab, slab)] = turned.reshape(slab, HD)
    for copy in k_copies + v_copies:
        copy.wait()

    width = cache_len + PAD
    scale = HD ** (-0.5)
    spot = lax.broadcasted_iota(jnp.int32, (NEW * GROUP, width), 1)
    token = lax.broadcasted_iota(jnp.int32, (NEW * GROUP, width), 0) // GROUP

    def attend_row(r, carry):
        first = cache_len + NEW * r
        valid = (spot < lengths[r]) | ((spot >= first) & (spot <= first + token))
        for g in range(KVH):
            q = jnp.concatenate(
                [qf[pl.ds(g * GROUP * OWN + NEW * r + j, GROUP, stride=OWN)] for j in range(NEW)],
                axis=0,
            ).astype(BF16)
            keys = kbuf[r, :, g * HD : (g + 1) * HD]
            scores = lax.dot_general(
                q, keys, (((1,), (1,)), ((), ())), preferred_element_type=F32
            )
            scores = jnp.where(valid, scores * scale, -1e30)
            top = jnp.max(scores, axis=-1, keepdims=True)
            weights = jnp.where(valid, jnp.exp(scores - top), 0.0).astype(BF16)
            below = jnp.sum(weights.astype(F32), axis=-1, keepdims=True)
            values = vbuf[r, :, g * HD : (g + 1) * HD]
            above = jnp.dot(weights, values, preferred_element_type=F32)
            result = above / below
            for j in range(NEW):
                af[pl.ds(g * GROUP * OWN + NEW * r + j, GROUP, stride=OWN)] = result[
                    j * GROUP : (j + 1) * GROUP
                ]
        return carry

    lax.fori_loop(0, ROW_DEV, attend_row, 0, unroll=UA)

    for d in range(tp):
        asend[d] = af[pl.ds(d * slab, slab)].astype(BF16)
    for step in range(1, tp):
        to = lax.rem(me + step, tp)
        copy = remote(asend.at[to], ar.at[me], aa_sem, (step,), to)
        copy.start()
        sends.append(copy)
    ar[me] = asend[me]
    for copy in o_copies:
        copy.wait()
    for step in range(1, tp):
        source = lax.rem(me + tp - step, tp)
        remote(asend.at[source], ar.at[source], aa_sem, (step,), source).wait_recv()

    order = [y * 2 + c for c in range(2) for y in range(ny)]
    heads = [ar[s].astype(F32) for s in order]
    for i in range(hh):
        lhs = jnp.concatenate([h[i * OWN : (i + 1) * OWN] for h in heads], axis=0)
        xo[:, i * BLK : (i + 1) * BLK] = lhs.astype(BF16)

    pairs = DB // CHUNKS // 2
    side = ny * OWN

    def stage1(ch):
        return remote(pbuf.at[ch, 1 - mc], rbuf.at[ch], s1_sem, (ch,), other)

    def stage2(ch, step):
        to = lax.rem(my + step, ny)
        piece = sbuf.at[ch, pl.ds(pl.multiple_of(to * OWN, OWN), OWN)]
        return remote(piece, fbuf.at[ch, my], s2_sem, (ch, step), to * 2 + mc)

    def pass_on(ch):
        stage1(ch).wait_recv()
        sbuf[ch] = pbuf[ch, mc] + rbuf[ch]
        for step in range(1, ny):
            stage2(ch, step).start()

    def project(ch, carry):
        def one_pair(pair, inner):
            n = (ch * pairs + pair) * 2
            total = None
            ahead = [reached[i] for i in range(hh)]
            slots = []
            for a in range(2):
                for i in range(hh):
                    at = ahead[i]
                    hit = o_cols[i, jnp.minimum(at, KEEP - 1)] == n + a
                    slots.append(jnp.where(hit, i * KEEP + at, hh * KEEP))
                    ahead[i] = at + hit.astype(jnp.int32)
            wide_k = 2 if hh % 2 == 0 else 1
            for i in range(0, hh, wide_k):
                w = jnp.concatenate(
                    [
                        jnp.concatenate(
                            [wo[slots[a * hh + i + b]] for b in range(wide_k)], axis=0
                        )
                        for a in range(2)
                    ],
                    axis=1,
                )
                part = jnp.dot(
                    xo[:, i * BLK : (i + wide_k) * BLK], w, preferred_element_type=F32
                )
                total = part if total is None else total + part
            columns = pl.ds(pl.multiple_of(pair * 2 * BLK, 2 * BLK), 2 * BLK)
            for c in range(2):
                pbuf[ch, c, :, columns] = total[c * side : (c + 1) * side]
            for i in range(hh):
                reached[i] = ahead[i]
            return inner

        lax.fori_loop(0, pairs, one_pair, 0, unroll=UO)
        stage1(ch).start()

        @pl.when(ch > 0)
        def _():
            pass_on(ch - 1)

        return carry

    for i in range(hh):
        reached[i] = 0
    lax.fori_loop(0, CHUNKS, project, 0)
    pass_on(CHUNKS - 1)

    def finish(ch, carry):
        total = sbuf[ch, pl.ds(pl.multiple_of(my * OWN, OWN), OWN)]
        for step in range(1, ny):
            source = lax.rem(my + ny - step, ny)
            remote(
                sbuf.at[ch, pl.ds(0, OWN)], fbuf.at[ch, source], s2_sem, (ch, step), other
            ).wait_recv()
            total = total + fbuf[ch, source]
        wide_chunk = D // CHUNKS
        columns = pl.ds(pl.multiple_of(ch * wide_chunk, wide_chunk), wide_chunk)
        for r in range(ROW_DEV):
            out[r, :, columns] = total[r * NEW : (r + 1) * NEW].astype(BF16)
        return carry

    lax.fori_loop(0, CHUNKS, finish, 0)

    x1.wait_send()
    for copy in x2 + x3 + sends:
        copy.wait_send()

    def drain(ch, carry):
        stage1(ch).wait_send()
        for step in range(1, ny):
            stage2(ch, step).wait_send()
        return carry

    lax.fori_loop(0, CHUNKS, drain, 0)


def hand_over(attn, fresh, attn_out, fresh_out):
    attn_out[...] = attn[...]
    fresh_out[...] = fresh[...]


def on_device(
    tp,
    hidden_states,
    norm_gain,
    q_blocks,
    q_rows,
    kv_blocks,
    kv_rows,
    o_blocks,
    o_cols,
    key_cache,
    value_cache,
    lengths,
):
    hh = q_blocks.shape[0]
    entries = kv_blocks.shape[0]
    cache_len = key_cache.shape[1]
    ny = tp // 2
    vmem = pl.BlockSpec(memory_space=pltpu.VMEM)
    smem = pl.BlockSpec(memory_space=pltpu.SMEM)
    hbm = pl.BlockSpec(memory_space=pltpu.HBM)
    slab = hh * OWN
    cols = max(1, entries // KEEP)
    width = cache_len + PAD
    chunk = D // CHUNKS
    dma = pltpu.SemaphoreType.DMA
    results = pl.pallas_call(
        functools.partial(kernel, tp, hh, entries, cache_len),
        out_shape=(
            jax.ShapeDtypeStruct((ROW_DEV, NEW, D), BF16),
            jax.ShapeDtypeStruct((ROW_DEV, NEW, 2 * KVH * HD), BF16),
        ),
        in_specs=[smem] + [hbm] * 10,
        out_specs=(vmem, vmem),
        scratch_shapes=[
            pltpu.VMEM((hh, KEEP, BLK, BLK), BF16),
            pltpu.VMEM((entries, BLK, BLK), BF16),
            pltpu.VMEM((hh * KEEP + 1, BLK, BLK), BF16),
            pltpu.VMEM((ROW_DEV, width, KVH * HD), BF16),
            pltpu.VMEM((ROW_DEV, width, KVH * HD), BF16),
            pltpu.VMEM((tp, DB * OWN, BLK), BF16),
            pltpu.VMEM((ny, DB, 2 * OWN, BLK), BF16),
            pltpu.VMEM((tp, slab, HD), BF16),
            pltpu.VMEM((tp, slab, HD), BF16),
            pltpu.VMEM((tp * slab, HD), F32),
            pltpu.VMEM((tp, cols * OWN, BLK), F32),
            pltpu.VMEM((tp, cols * OWN, BLK), F32),
            pltpu.VMEM((tp * slab, HD), F32),
            pltpu.VMEM((tp, slab, HD), BF16),
            pltpu.VMEM((tp, slab, HD), BF16),
            pltpu.VMEM((tp * OWN, hh * BLK), BF16),
            pltpu.VMEM((CHUNKS, 2, ny * OWN, chunk), F32),
            pltpu.VMEM((CHUNKS, ny * OWN, chunk), F32),
            pltpu.VMEM((CHUNKS, ny * OWN, chunk), F32),
            pltpu.VMEM((CHUNKS, ny, OWN, chunk), F32),
            pltpu.SMEM((hh,), jnp.int32),
            pltpu.VMEM((ROW_DEV, NEW, D), BF16),
            pltpu.VMEM((D,), BF16),
            pltpu.SMEM((hh, KEEP), jnp.int32),
            pltpu.SMEM((entries,), jnp.int32),
            pltpu.SMEM((hh, KEEP), jnp.int32),
            dma((5,)),
            dma((hh,)),
            dma,
            dma((hh,)),
            dma((2, ROW_DEV)),
            dma((2, 1)),
            dma((2, ny, PIECES)),
            dma((2, ny, PIECES)),
            dma((2, tp)),
            dma((2, tp)),
            dma((2, tp)),
            dma((2, CHUNKS)),
            dma((2, CHUNKS, ny)),
        ],
        compiler_params=pltpu.CompilerParams(
            collective_id=0, has_side_effects=True, vmem_limit_bytes=60 * 1024 * 1024
        ),
    )(
        lengths,
        hidden_states,
        norm_gain,
        q_rows,
        kv_rows,
        o_cols,
        q_blocks,
        kv_blocks,
        o_blocks,
        key_cache,
        value_cache,
    )
    return pl.pallas_call(
        hand_over,
        out_shape=tuple(jax.ShapeDtypeStruct(r.shape, r.dtype) for r in results),
        in_specs=[vmem] * 2,
        out_specs=(vmem, vmem),
    )(*results)


def solution(mesh):
    rows = P(("groups", "tensor", "dp"), None, None)
    return jax.shard_map(
        functools.partial(on_device, mesh.shape["tensor"]),
        mesh=mesh,
        in_specs=(
            rows,
            P(),
            P("tensor", None, None, None),
            P("tensor", None),
            P("tensor", None, None),
            P("tensor"),
            P("tensor", None, None, None),
            P("tensor", None),
            rows,
            rows,
            P(("groups", "tensor", "dp")),
        ),
        out_specs=(rows, rows),
        check_vma=False,
    )
```
